32 devices in a mesh: blk: 8 (over y, x, core), view: 4 (over z).
Axes of the slice: x: 2, y: 2, z: 4, core: 2. Of those that a mesh axis runs over, the one named last changes fastest.
Arguments:
- estimate: float32 [256, 128, 128], P('blk'), may hold values from 0.5 to 1.5
- observed: bfloat16 [4, 256, 128, 128], P('view', 'blk'), may hold values from 0.19921875 to 2
- psf_taps: float32 [4, 2, 3, 31], P('view'), may hold values from 0.05 to 1
- psf_weight: float32 [4, 2], P('view'), may hold values from 0.2 to 1
- shifts: int32 [4, 3], P('view'), may hold values from -8 to 8, as said below
- cover_first: int32 [4], replicated, may hold values from 0 to 6, as said below
- cover_count: int32 [4], replicated, may hold values from 2 to 8, as said below
Outputs:
- joined: float32 [256, 128, 128], P('blk')
The draws below stay inside these ranges and needn't reach their ends.
Inputs may be any that keep to these rules, and one draw needn't show every extreme that they name: `shifts`: every component of a registration shift lies in -8 .. 8; some view that covers every block has first component 8, and another that covers every block has -8. View v covers the whole blocks cover_first[v] .. cover_first[v] + cover_count[v] - 1, all inside the volume; two or more views cover every block, and some view covers only the last 2 blocks. `cover_count`: together with cover_first, the covered blocks of each view lie within the volume.
All inputs are finite; a program needn't handle non-finite values.
Results may differ from the reference program's by a relative error of at most 0.0003.
Values may be sent and summed in bfloat16 or wider, within the bound.
A program may use at most 128 MiB of HBM per device.

```python
import math
import jax
import jax.numpy as jnp
from jax import lax

PLANES = 32
ROWS_Y = 128
COLS_Z = 128
TAPS = 31
SHIFT_MAX = 8
ROUNDS = 2
HALF_TAPS = 15
VIEWS = 4
SLAB_X = 256


def view_order(key):
    return jax.random.permutation(jax.random.fold_in(key, 11), VIEWS)


def cover_table(key):
    blocks = SLAB_X // PLANES
    shortest = max(blocks // 4, 1)
    order = view_order(key)
    key_count, key_first = jax.random.split(jax.random.fold_in(key, 13))
    counts = jax.random.randint(key_count, (VIEWS,), shortest, blocks + 1)
    slots = jnp.arange(VIEWS)
    counts = jnp.where(slots == order[0], blocks, counts)
    counts = jnp.where(slots == order[2], blocks, counts)
    counts = jnp.where(slots == order[1], shortest, counts).astype(jnp.int32)
    firsts = jax.random.randint(key_first, (VIEWS,), 0, blocks - counts + 1)
    firsts = jnp.where(slots == order[1], blocks - shortest, firsts).astype(jnp.int32)
    return (firsts, counts)


def draw_cover_first(key, part):
    firsts, counts = cover_table(key)
    return firsts


def draw_cover_count(key, part):
    firsts, counts = cover_table(key)
    return counts


def draw_shifts(key, part):
    order = view_order(key)
    key = jax.random.fold_in(key, 7)
    values = jax.random.randint(key, (VIEWS, 3), -SHIFT_MAX, SHIFT_MAX + 1)
    values = values.at[order[0], 0].set(SHIFT_MAX)
    values = values.at[order[2], 0].set(-SHIFT_MAX)
    return values.astype(jnp.int32)


def block_levels(own_key, shape, shards, smallest, high):
    level, own = 1.0, jax.random.fold_in(own_key, 6)
    for position, parts in shards:
        steps = jnp.exp(jax.random.uniform(jax.random.fold_in(own, position), (parts,), jnp.float32, smallest / len(shards), high / len(shards)))
        level = level * jnp.repeat(steps, shape[position] // parts).reshape([-1 if axis == position else 1 for axis in range(len(shape))])
    return level


def setup_inputs(seed: int = 0) -> dict:
    key_of = jax.random.split(jax.random.key(seed), 8)
    return {
        "estimate": jnp.clip(0.5 + 1.0 * jax.random.uniform(key_of[0], (SLAB_X, ROWS_Y, COLS_Z), jnp.float32) ** block_levels(key_of[0], (SLAB_X, ROWS_Y, COLS_Z), ((0, 8),), -0.2, 0.2), 0.5, 1.5),
        "observed": jnp.clip(0.19921875 + 1.8007812 * jax.random.uniform(key_of[1], (VIEWS, SLAB_X, ROWS_Y, COLS_Z), jnp.float32) ** block_levels(key_of[1], (VIEWS, SLAB_X, ROWS_Y, COLS_Z), ((0, 4), (1, 8)), -0.2, 0.2), 0.19921875, 2.0).astype(jnp.bfloat16),
        "psf_taps": jnp.clip(jnp.exp(math.log(1.0) - 2.9957323 * jax.random.uniform(key_of[2], (VIEWS, 2, 3, TAPS), jnp.float32) ** block_levels(key_of[2], (VIEWS, 2, 3, TAPS), ((0, 4),), -0.2, 0.2)), 0.05, 1.0),
        "psf_weight": jnp.clip(jnp.exp(math.log(1.0) - 1.609438 * jax.random.uniform(key_of[3], (VIEWS, 2), jnp.float32) ** block_levels(key_of[3], (VIEWS, 2), ((0, 4),), -0.2, 0.2)), 0.2, 1.0),
        "shifts": draw_shifts(jax.random.fold_in(key_of[7], 71), 0),
        "cover_first": draw_cover_first(jax.random.fold_in(key_of[7], 71), 0),
        "cover_count": draw_cover_count(jax.random.fold_in(key_of[7], 71), 0),
    }


OFFSET = 0.1


def band_matrix(taps, rows, cols, offset):
    diff = lax.broadcasted_iota(jnp.int32, (rows, cols), 1) - lax.broadcasted_iota(jnp.int32, (rows, cols), 0) + offset
    matrix = jnp.zeros((rows, cols), jnp.float32)
    for place in range(taps.shape[0]):
        matrix = matrix + jnp.where(diff == place, taps[place], jnp.float32(0.0))
    return matrix


def band_set(taps, planes, rows, cols, half):
    result = []
    for rank in range(2):
        result.append((band_matrix(taps[rank, 0], planes, planes + 2 * half, 0),
                       band_matrix(taps[rank, 1], rows, rows, half),
                       band_matrix(taps[rank, 2], cols, cols, half)))
    return result


def blur_block(window, mats, weights):
    total = None
    for rank in range(2):
        mat_x, mat_y, mat_z = mats[rank]
        part = jnp.einsum("ij,jyz->iyz", mat_x, window, precision=lax.Precision.HIGHEST)
        part = jnp.einsum("ij,xjz->xiz", mat_y, part, precision=lax.Precision.HIGHEST)
        part = jnp.einsum("ij,xyj->xyi", mat_z, part, precision=lax.Precision.HIGHEST)
        term = weights[rank] * part
        total = term if total is None else total + term
    return total


def blur_volume(field, mats, weights):
    blocks = field.reshape(SLAB_X // PLANES, PLANES, ROWS_Y, COLS_Z)
    zeros = jnp.zeros((1, PLANES, ROWS_Y, COLS_Z), field.dtype)
    before = jnp.concatenate([zeros, blocks[:-1]], 0)[:, PLANES - HALF_TAPS:]
    after = jnp.concatenate([blocks[1:], zeros], 0)[:, :HALF_TAPS]
    windows = jnp.concatenate([before, blocks, after], 1)

    def one_block(window):
        return blur_block(window, mats, weights)

    return lax.map(one_block, windows).reshape(field.shape)


def reference(estimate, observed, psf_taps, psf_weight, shifts, cover_first, cover_count):
    block_of = lax.broadcasted_iota(jnp.int32, (SLAB_X,), 0) // PLANES
    inside = (block_of[None, :] >= cover_first[:, None]) & (block_of[None, :] < (cover_first + cover_count)[:, None])
    masks = jnp.where(inside, 1.0, 0.0).astype(jnp.float32)
    covered = jnp.sum(masks, 0)
    shares = masks / covered
    padded_obs = jnp.pad(observed, ((0, 0), (SHIFT_MAX, SHIFT_MAX), (SHIFT_MAX, SHIFT_MAX), (SHIFT_MAX, SHIFT_MAX)))
    registered = []
    for view in range(VIEWS):
        start = (SHIFT_MAX + shifts[view, 0], SHIFT_MAX + shifts[view, 1], SHIFT_MAX + shifts[view, 2])
        piece = lax.dynamic_slice(padded_obs[view], start, (SLAB_X, ROWS_Y, COLS_Z))
        registered.append(piece.astype(jnp.float32))
    taps = psf_taps / jnp.sum(psf_taps, axis=-1, keepdims=True)
    weights = psf_weight / jnp.sum(psf_weight, axis=-1, keepdims=True)
    forward = [band_set(taps[view], PLANES, ROWS_Y, COLS_Z, HALF_TAPS) for view in range(VIEWS)]
    backward = [band_set(taps[view][:, :, ::-1], PLANES, ROWS_Y, COLS_Z, HALF_TAPS) for view in range(VIEWS)]
    field = estimate
    for step in range(ROUNDS):
        exponent = jnp.zeros_like(field)
        for view in range(VIEWS):
            blurred = blur_volume(field, forward[view], weights[view])
            ratio = (registered[view] + OFFSET) / (blurred + OFFSET)
            correction = blur_volume(ratio, backward[view], weights[view])
            exponent = exponent + shares[view][:, None, None] * jnp.log(correction)
        field = field * jnp.exp(exponent)
    return field
```

```python
import functools

import jax
import jax.numpy as jnp
from jax import lax
from jax.experimental import pallas as pl
from jax.experimental.pallas import tpu as pltpu
from jax.sharding import PartitionSpec as P

SHIFT_MAX = 8
ROUNDS = 2
HALF_TAPS = 15
HALO = 16
OFFSET = 0.1
GROUP = 16


def halo(block, axis, dim, width):
    count = lax.axis_size(axis)
    forward = [(i, i + 1) for i in range(count - 1)]
    backward = [(target, source) for source, target in forward]
    low = lax.ppermute(
        lax.slice_in_dim(block, block.shape[dim] - width, None, axis=dim), axis, forward
    )
    high = lax.ppermute(lax.slice_in_dim(block, 0, width, axis=dim), axis, backward)
    return low, high


def split(value):
    high = value.astype(jnp.bfloat16)
    low = (value - high.astype(jnp.float32)).astype(jnp.bfloat16)
    return high, low


def dot(a, b):
    return jnp.dot(a, b, preferred_element_type=jnp.float32)


def band(taps, rank, factor, diff, reverse):
    count = taps.shape[2]
    matrix = jnp.zeros(diff.shape, jnp.float32)
    total = jnp.float32(0.0)
    for place in range(count):
        tap = taps[rank, factor, count - 1 - place if reverse else place]
        total = total + tap
        matrix = jnp.where(diff == place, tap, matrix)
    return matrix / jnp.full(diff.shape, total, jnp.float32)


def iota(shape, dim):
    return lax.broadcasted_iota(jnp.int32, shape, dim)


def blur_tables(taps, weight, planes, width, rows, cols, reverse, mat_x, mat_y, mat_z):
    half = HALF_TAPS
    weight_sum = weight[0] + weight[1]
    shape = (planes, 4 * width)
    part = iota(shape, 1) // width
    diff = iota(shape, 1) % width - iota(shape, 0) - (HALO - half)
    for rank in range(2):
        scale = jnp.full(shape, weight[rank], jnp.float32) / jnp.full(shape, weight_sum, jnp.float32)
        full = band(taps, rank, 0, diff, reverse) * scale
        high = full.astype(jnp.bfloat16).astype(jnp.float32)
        mixed = jnp.where(part < 2, high, jnp.where(part == 2, full - high, 0.0))
        mat_x[rank * planes : (rank + 1) * planes, :] = mixed.astype(jnp.bfloat16)
        shape_y = (rows, rows)
        high, low = split(
            band(taps, rank, 1, iota(shape_y, 1) - iota(shape_y, 0) + half, reverse)
        )
        mat_y[:rows, rank * rows : (rank + 1) * rows] = high
        mat_y[rows:, rank * rows : (rank + 1) * rows] = low
        shape_z = (cols, cols)
        high, low = split(
            band(taps, rank, 2, iota(shape_z, 0) - iota(shape_z, 1) + half, reverse)
        )
        for copy in range(2):
            mat_z[rank, copy * cols : (copy + 1) * cols, :cols] = high
            mat_z[rank, copy * cols : (copy + 1) * cols, cols:] = low


def blur(window, middle, mat_x, mat_y, mat_z, planes, width, rows, cols, finish):
    def first(step, carry):
        base = step * GROUP
        parts = []
        for k in range(GROUP // 2):
            sides = []
            for side in range(2):
                y = base + 2 * k + side
                high, low = split(window[pl.ds(y, width, stride=rows), :])
                sides.append(jnp.concatenate([high, low, high], axis=0))
            both = dot(mat_x[:, : 3 * width], jnp.concatenate(sides, axis=1))
            parts.append(both[:, :cols])
            parts.append(both[:, cols:])
        for rank in range(2):
            stack = jnp.concatenate(
                [p[rank * planes : (rank + 1) * planes] for p in parts], axis=0
            )
            high, low = split(stack)
            both = dot(jnp.concatenate([high, low], axis=1), mat_z[rank])
            result = both[:, :cols] + both[:, cols:]
            for k in range(GROUP):
                middle[pl.ds(rank * planes * rows + base + k, planes, stride=rows), :] = result[
                    k * planes : (k + 1) * planes
                ]
        return carry

    lax.fori_loop(0, rows // GROUP, first, 0)

    def second(step, carry):
        x = 2 * step
        highs, lows = [], []
        for side in range(2):
            data = [
                middle[pl.ds(pl.multiple_of((rank * planes + x + side) * rows, 8), rows), :]
                for rank in range(2)
            ]
            high, low = split(jnp.concatenate(data, axis=0))
            highs.append(high)
            lows.append(low)
        both = dot(mat_y[...], jnp.concatenate(highs, axis=1))
        result = both[:rows] + both[rows:]
        result = result + dot(mat_y[:rows, :], jnp.concatenate(lows, axis=1))
        finish(x, result[:, :cols])
        finish(x + 1, result[:, cols:])
        return carry

    lax.fori_loop(0, planes // 2, second, 0)


def load_window(low, own, high, window, planes, rows, cols):
    size = HALO * rows
    window[:size, :] = low[...].astype(jnp.float32).reshape(size, cols)
    window[size : size + planes * rows, :] = own[...].reshape(planes * rows, cols)
    window[size + planes * rows :, :] = high[...].astype(jnp.float32).reshape(size, cols)


def forward_kernel(taps, weight, low, own, high, registered, out, window, middle, mx, my, mz):
    planes, rows, cols = own.shape
    width = planes + 2 * HALO
    blur_tables(taps, weight, planes, width, rows, cols, False, mx, my, mz)
    load_window(low, own, high, window, planes, rows, cols)

    def finish(x, value):
        out[x] = (registered[x].astype(jnp.float32) + OFFSET) / (value + OFFSET)

    blur(window, middle, mx, my, mz, planes, width, rows, cols, finish)


def backward_kernel(
    taps, weight, first, count, low, own, high, out, window, middle, mx, my, mz
):
    planes, rows, cols = own.shape
    width = planes + 2 * HALO
    blur_tables(taps, weight, planes, width, rows, cols, True, mx, my, mz)
    load_window(low, own, high, window, planes, rows, cols)
    view = lax.axis_index("view")
    block = lax.axis_index("blk")
    covered = jnp.float32(0.0)
    owned = jnp.float32(0.0)
    for slot in range(first.shape[0]):
        inside = (block >= first[slot]) & (block < first[slot] + count[slot])
        covered = covered + jnp.where(inside, 1.0, 0.0)
        owned = owned + jnp.where(inside & (view == slot), 1.0, 0.0)
    share = jnp.full((rows, cols), owned, jnp.float32) / jnp.full((rows, cols), covered, jnp.float32)

    def finish(x, value):
        out[x] = share * jnp.log(value)

    blur(window, middle, mx, my, mz, planes, width, rows, cols, finish)


def call(kernel, scalars, arrays, shape):
    planes, rows, cols = shape
    width = planes + 2 * HALO
    return pl.pallas_call(
        kernel,
        out_shape=jax.ShapeDtypeStruct(shape, jnp.float32),
        in_specs=[pl.BlockSpec(memory_space=pltpu.SMEM)] * len(scalars)
        + [pl.BlockSpec(memory_space=pltpu.VMEM)] * len(arrays),
        out_specs=pl.BlockSpec(memory_space=pltpu.VMEM),
        scratch_shapes=[
            pltpu.VMEM((width * rows, cols), jnp.float32),
            pltpu.VMEM((2 * planes * rows, cols), jnp.float32),
            pltpu.VMEM((2 * planes, 4 * width), jnp.bfloat16),
            pltpu.VMEM((2 * rows, 2 * rows), jnp.bfloat16),
            pltpu.VMEM((2, 2 * cols, 2 * cols), jnp.bfloat16),
        ],
        compiler_params=pltpu.CompilerParams(vmem_limit_bytes=40 * 2**20),
        cost_estimate=pl.CostEstimate(
            flops=12 * planes * rows * cols * 3 * cols,
            bytes_accessed=12 * planes * rows * cols,
            transcendentals=0,
        ),
    )(*scalars, *arrays)


def on_device(estimate, observed, psf_taps, psf_weight, shifts, cover_first, cover_count):
    planes, rows, cols = estimate.shape
    taps, weight = psf_taps[0], psf_weight[0]
    field_low, field_high = halo(estimate.astype(jnp.bfloat16), "blk", 0, HALO)
    low, high = halo(observed[0], "blk", 0, SHIFT_MAX)
    extended = jnp.concatenate([low, observed[0], high], axis=0)
    extended = jnp.pad(extended, ((0, 0), (SHIFT_MAX, SHIFT_MAX), (SHIFT_MAX, SHIFT_MAX)))
    start = (SHIFT_MAX + shifts[0, 0], SHIFT_MAX + shifts[0, 1], SHIFT_MAX + shifts[0, 2])
    registered = lax.dynamic_slice(extended, start, (planes, rows, cols))
    field = estimate
    for step in range(ROUNDS):
        if step:
            field_low, field_high = halo(field.astype(jnp.bfloat16), "blk", 0, HALO)
        ratio = call(
            forward_kernel,
            (taps, weight),
            (field_low, field, field_high, registered),
            estimate.shape,
        )
        ratio_low, ratio_high = halo(ratio.astype(jnp.bfloat16), "blk", 0, HALO)
        weighted_log = call(
            backward_kernel,
            (taps, weight, cover_first, cover_count),
            (ratio_low, ratio, ratio_high),
            estimate.shape,
        )
        field = field * jnp.exp(lax.psum(weighted_log, "view"))
    return field


def solution(mesh):
    placed = (
        P("blk", None, None),
        P("view", "blk", None, None),
        P("view", None, None, None),
        P("view", None),
        P("view", None),
        P(),
        P(),
    )
    return jax.shard_map(
        on_device, mesh=mesh, in_specs=placed, out_specs=P("blk", None, None), check_vma=False
    )
```

```python
import math

import jax
import jax.numpy as jnp
from jax import lax
from jax.experimental import pallas as pl
from jax.experimental.pallas import tpu as pltpu
from jax.sharding import PartitionSpec as P

SHIFT_MAX = 8
ROUNDS = 2
HALF_TAPS = 15
HALO = 16
OFFSET = 0.1
GROUP = 16
CHUNKS = 4
KNEE = 0.05
LIMIT = 24.0
UNIT = math.log(1.0 + LIMIT / KNEE) / 32767.0


def halo(block, axis, dim, width):
    count = lax.axis_size(axis)
    forward = [(i, i + 1) for i in range(count - 1)]
    backward = [(target, source) for source, target in forward]
    low = lax.ppermute(
        lax.slice_in_dim(block, block.shape[dim] - width, None, axis=dim), axis, forward
    )
    high = lax.ppermute(lax.slice_in_dim(block, 0, width, axis=dim), axis, backward)
    return low, high


def split(value):
    high = value.astype(jnp.bfloat16)
    low = (value - high.astype(jnp.float32)).astype(jnp.bfloat16)
    return high, low


def dot(a, b):
    return jnp.dot(a, b, preferred_element_type=jnp.float32)


def band(taps, rank, factor, diff, reverse):
    count = taps.shape[2]
    matrix = jnp.zeros(diff.shape, jnp.float32)
    total = jnp.float32(0.0)
    for place in range(count):
        tap = taps[rank, factor, count - 1 - place if reverse else place]
        total = total + tap
        matrix = jnp.where(diff == place, tap, matrix)
    return matrix / jnp.full(diff.shape, total, jnp.float32)


def iota(shape, dim):
    return lax.broadcasted_iota(jnp.int32, shape, dim)


def blur_tables(taps, weight, planes, width, rows, cols, reverse, mat_x, mat_y, mat_z):
    half = HALF_TAPS
    weight_sum = weight[0] + weight[1]
    shape = (planes, 4 * width)
    part = iota(shape, 1) // width
    diff = iota(shape, 1) % width - iota(shape, 0) - (HALO - half)
    for rank in range(2):
        scale = jnp.full(shape, weight[rank], jnp.float32) / jnp.full(shape, weight_sum, jnp.float32)
        full = band(taps, rank, 0, diff, reverse) * scale
        high = full.astype(jnp.bfloat16).astype(jnp.float32)
        mixed = jnp.where(part < 2, high, jnp.where(part == 2, full - high, 0.0))
        mat_x[rank * planes : (rank + 1) * planes, :] = mixed.astype(jnp.bfloat16)
        shape_y = (rows, rows)
        high, low = split(
            band(taps, rank, 1, iota(shape_y, 1) - iota(shape_y, 0) + half, reverse)
        )
        mat_y[:rows, rank * rows : (rank + 1) * rows] = high
        mat_y[rows:, rank * rows : (rank + 1) * rows] = low
        shape_z = (cols, cols)
        high, low = split(
            band(taps, rank, 2, iota(shape_z, 0) - iota(shape_z, 1) + half, reverse)
        )
        for copy in range(2):
            mat_z[rank, copy * cols : (copy + 1) * cols, :cols] = high
            mat_z[rank, copy * cols : (copy + 1) * cols, cols:] = low


def blur_xz(window, middle, mat_x, mat_z, planes, width, rows, cols):
    def first(step, carry):
        base = step * GROUP
        parts = []
        for k in range(GROUP // 2):
            sides = []
            for side in range(2):
                y = base + 2 * k + side
                high, low = split(window[pl.ds(y, width, stride=rows), :])
                sides.append(jnp.concatenate([high, low, high], axis=0))
            both = dot(mat_x[:, : 3 * width], jnp.concatenate(sides, axis=1))
            parts.append(both[:, :cols])
            parts.append(both[:, cols:])
        for rank in range(2):
            stack = jnp.concatenate(
                [p[rank * planes : (rank + 1) * planes] for p in parts], axis=0
            )
            high, low = split(stack)
            both = dot(jnp.concatenate([high, low], axis=1), mat_z[rank])
            result = both[:, :cols] + both[:, cols:]
            for k in range(GROUP):
                middle[pl.ds(rank * planes * rows + base + k, planes, stride=rows), :] = result[
                    k * planes : (k + 1) * planes
                ]
        return carry

    lax.fori_loop(0, rows // GROUP, first, 0)


def blur_y(middle, mat_y, planes, rows, cols, start, number, finish):
    def second(step, carry):
        x = start + 2 * step
        highs, lows = [], []
        for side in range(2):
            data = [
                middle[pl.ds(pl.multiple_of((rank * planes + x + side) * rows, 8), rows), :]
                for rank in range(2)
            ]
            high, low = split(jnp.concatenate(data, axis=0))
            highs.append(high)
            lows.append(low)
        both = dot(mat_y[...], jnp.concatenate(highs, axis=1))
        result = both[:rows] + both[rows:]
        result = result + dot(mat_y[:rows, :], jnp.concatenate(lows, axis=1))
        finish(2 * step, result[:, :cols])
        finish(2 * step + 1, result[:, cols:])
        return carry

    lax.fori_loop(0, number // 2, second, 0)


def load_window(low, own, high, window, planes, rows, cols):
    size = HALO * rows
    window[:size, :] = low[...].astype(jnp.float32).reshape(size, cols)
    window[size : size + planes * rows, :] = own[...].reshape(planes * rows, cols)
    window[size + planes * rows :, :] = high[...].astype(jnp.float32).reshape(size, cols)


def forward_kernel(taps, weight, low, own, high, registered, out, window, middle, mx, my, mz):
    planes, rows, cols = own.shape
    width = planes + 2 * HALO
    blur_tables(taps, weight, planes, width, rows, cols, False, mx, my, mz)
    load_window(low, own, high, window, planes, rows, cols)

    def finish(x, value):
        out[x] = (registered[x].astype(jnp.float32) + OFFSET) / (value + OFFSET)

    blur_xz(window, middle, mx, mz, planes, width, rows, cols)
    blur_y(middle, my, planes, rows, cols, 0, planes, finish)


def encode(value):
    size = jnp.log(1.0 + jnp.abs(value) * (1.0 / KNEE)) * (1.0 / UNIT) + 0.5
    size = jnp.minimum(size, 32767.0)
    return jnp.where(value < 0.0, -size, size).astype(jnp.int32).astype(jnp.int16)


def decode(code):
    value = code.astype(jnp.int32).astype(jnp.float32)
    size = KNEE * (jnp.exp(UNIT * jnp.abs(value)) - 1.0)
    return jnp.where(value < 0.0, -size, size)


def backward_kernel(
    taps, weight, first, count, low, own, high, field, out, window, middle, mx, my, mz,
    mine, send, recv, send_sems, recv_sems,
):
    planes, rows, cols = own.shape
    width = planes + 2 * HALO
    view = lax.axis_index("view")
    block = lax.axis_index("blk")
    side = lax.rem(view, 2)
    partner = view + 1 - 2 * side
    across = lax.rem(view + 2, 4)
    barrier = pltpu.get_barrier_semaphore()
    for other in (partner, across):
        pl.semaphore_signal(
            barrier, inc=1, device_id={"view": other}, device_id_type=pl.DeviceIdType.MESH
        )

    blur_tables(taps, weight, planes, width, rows, cols, True, mx, my, mz)
    load_window(low, own, high, window, planes, rows, cols)
    covered = jnp.float32(0.0)
    owned = jnp.float32(0.0)
    for slot in range(first.shape[0]):
        inside = (block >= first[slot]) & (block < first[slot] + count[slot])
        covered = covered + jnp.where(inside, 1.0, 0.0)
        owned = owned + jnp.where(inside & (view == slot), 1.0, 0.0)
    share = jnp.full((rows, cols), owned, jnp.float32) / jnp.full((rows, cols), covered, jnp.float32)

    blur_xz(window, middle, mx, mz, planes, width, rows, cols)
    pl.semaphore_wait(barrier, 2)

    half = planes // (2 * CHUNKS)

    def copy(stage, chunk):
        return pltpu.make_async_remote_copy(
            src_ref=send.at[stage, chunk],
            dst_ref=recv.at[stage, chunk],
            send_sem=send_sems.at[stage, chunk],
            recv_sem=recv_sems.at[stage, chunk],
            device_id={"view": across if stage == 1 else partner},
            device_id_type=pl.DeviceIdType.MESH,
        )

    def produce(chunk):
        base = chunk * 2 * half

        def give(place, value):
            send[0, chunk, place] = encode(share * jnp.log(value))

        blur_y(middle, my, planes, rows, cols, base + (1 - side) * half, half, give)
        copy(0, chunk).start()

        def keep(place, value):
            mine[chunk, place] = share * jnp.log(value)

        blur_y(middle, my, planes, rows, cols, base + side * half, half, keep)

    def add_pair(chunk):
        copy(0, chunk).wait_recv()

        def body(place, carry):
            send[1, chunk, place] = encode(mine[chunk, place] + decode(recv[0, chunk, place]))
            return carry

        lax.fori_loop(0, half, body, 0)
        copy(1, chunk).start()

    def update(chunk, place, which, code):
        x = chunk * 2 * half + which * half + place
        out[x] = field[x] * jnp.exp(decode(code))

    def add_across(chunk):
        copy(1, chunk).wait_recv()

        def body(place, carry):
            total = encode(decode(send[1, chunk, place]) + decode(recv[1, chunk, place]))
            send[2, chunk, place] = total
            update(chunk, place, side, total)
            return carry

        lax.fori_loop(0, half, body, 0)
        copy(2, chunk).start()

    def take(chunk):
        copy(2, chunk).wait_recv()

        def body(place, carry):
            update(chunk, place, 1 - side, recv[2, chunk, place])
            return carry

        lax.fori_loop(0, half, body, 0)

    for chunk in range(CHUNKS):
        produce(chunk)
        if chunk:
            add_pair(chunk - 1)
    add_pair(CHUNKS - 1)
    for chunk in range(CHUNKS):
        add_across(chunk)
        if chunk:
            take(chunk - 1)
    take(CHUNKS - 1)
    for stage in range(3):
        for chunk in range(CHUNKS):
            copy(stage, chunk).wait_send()


def call(kernel, scalars, arrays, shape, scratch=(), **params):
    planes, rows, cols = shape
    width = planes + 2 * HALO
    return pl.pallas_call(
        kernel,
        out_shape=jax.ShapeDtypeStruct(shape, jnp.float32),
        in_specs=[pl.BlockSpec(memory_space=pltpu.SMEM)] * len(scalars)
        + [pl.BlockSpec(memory_space=pltpu.VMEM)] * len(arrays),
        out_specs=pl.BlockSpec(memory_space=pltpu.VMEM),
        scratch_shapes=[
            pltpu.VMEM((width * rows, cols), jnp.float32),
            pltpu.VMEM((2 * planes * rows, cols), jnp.float32),
            pltpu.VMEM((2 * planes, 4 * width), jnp.bfloat16),
            pltpu.VMEM((2 * rows, 2 * rows), jnp.bfloat16),
            pltpu.VMEM((2, 2 * cols, 2 * cols), jnp.bfloat16),
            *scratch,
        ],
        compiler_params=pltpu.CompilerParams(vmem_limit_bytes=40 * 2**20, **params),
        cost_estimate=pl.CostEstimate(
            flops=12 * planes * rows * cols * 3 * cols,
            bytes_accessed=12 * planes * rows * cols,
            transcendentals=0,
        ),
    )(*scalars, *arrays)


def on_device(estimate, observed, psf_taps, psf_weight, shifts, cover_first, cover_count):
    planes, rows, cols = estimate.shape
    taps, weight = psf_taps[0], psf_weight[0]
    field_low, field_high = halo(estimate.astype(jnp.bfloat16), "blk", 0, HALO)
    low, high = halo(observed[0], "blk", 0, SHIFT_MAX)
    extended = jnp.concatenate([low, observed[0], high], axis=0)
    extended = jnp.pad(extended, ((0, 0), (SHIFT_MAX, SHIFT_MAX), (SHIFT_MAX, SHIFT_MAX)))
    start = (SHIFT_MAX + shifts[0, 0], SHIFT_MAX + shifts[0, 1], SHIFT_MAX + shifts[0, 2])
    registered = lax.dynamic_slice(extended, start, (planes, rows, cols))
    field = estimate
    for step in range(ROUNDS):
        if step:
            field_low, field_high = halo(field.astype(jnp.bfloat16), "blk", 0, HALO)
        ratio = call(
            forward_kernel,
            (taps, weight),
            (field_low, field, field_high, registered),
            estimate.shape,
        )
        ratio_low, ratio_high = halo(ratio.astype(jnp.bfloat16), "blk", 0, HALO)
        chunk = (CHUNKS, planes // (2 * CHUNKS), rows, cols)
        field = call(
            backward_kernel,
            (taps, weight, cover_first, cover_count),
            (ratio_low, ratio, ratio_high, field),
            estimate.shape,
            (
                pltpu.VMEM(chunk, jnp.float32),
                pltpu.VMEM((3, *chunk), jnp.int16),
                pltpu.VMEM((3, *chunk), jnp.int16),
                pltpu.SemaphoreType.DMA((3, CHUNKS)),
                pltpu.SemaphoreType.DMA((3, CHUNKS)),
            ),
            collective_id=0,
            has_side_effects=True,
        )
    return field


def solution(mesh):
    placed = (
        P("blk", None, None),
        P("view", "blk", None, None),
        P("view", None, None, None),
        P("view", None),
        P("view", None),
        P(),
        P(),
    )
    return jax.shard_map(
        on_device, mesh=mesh, in_specs=placed, out_specs=P("blk", None, None), check_vma=False
    )
```

```python
import math

import jax
import jax.numpy as jnp
from jax import lax
from jax.experimental import pallas as pl
from jax.experimental.pallas import tpu as pltpu
from jax.sharding import PartitionSpec as P

SHIFT_MAX = 8
ROUNDS = 2
HALF_TAPS = 15
HALO = 16
OFFSET = 0.1
GROUP = 16
CHUNK = 4
PIECE = 8
KNEE = 0.05
LIMIT = 24.0
UNIT = math.log(1.0 + LIMIT / KNEE) / 32767.0


def split(value):
    high = value.astype(jnp.bfloat16)
    low = (value - high.astype(jnp.float32)).astype(jnp.bfloat16)
    return high, low


def dot(a, b):
    return jnp.dot(a, b, preferred_element_type=jnp.float32)


def band(taps, rank, factor, diff, reverse):
    count = taps.shape[2]
    matrix = jnp.zeros(diff.shape, jnp.float32)
    total = jnp.float32(0.0)
    for place in range(count):
        tap = taps[rank, factor, count - 1 - place if reverse else place]
        total = total + tap
        matrix = jnp.where(diff == place, tap, matrix)
    return matrix / jnp.full(diff.shape, total, jnp.float32)


def iota(shape, dim):
    return lax.broadcasted_iota(jnp.int32, shape, dim)


def blur_tables(taps, weight, planes, width, rows, cols, reverse, mat_x, mat_y, mat_z):
    half = HALF_TAPS
    weight_sum = weight[0] + weight[1]
    shape = (planes, 4 * width)
    part = iota(shape, 1) // width
    diff = iota(shape, 1) % width - iota(shape, 0) - (HALO - half)
    for rank in range(2):
        scale = jnp.full(shape, weight[rank], jnp.float32) / jnp.full(shape, weight_sum, jnp.float32)
        full = band(taps, rank, 0, diff, reverse) * scale
        high = full.astype(jnp.bfloat16).astype(jnp.float32)
        mixed = jnp.where(part < 2, high, jnp.where(part == 2, full - high, 0.0))
        mat_x[rank * planes : (rank + 1) * planes, :] = mixed.astype(jnp.bfloat16)
        shape_y = (rows, rows)
        high, low = split(
            band(taps, rank, 1, iota(shape_y, 1) - iota(shape_y, 0) + half, reverse)
        )
        mat_y[:rows, rank * rows : (rank + 1) * rows] = high
        mat_y[rows:, rank * rows : (rank + 1) * rows] = low
        shape_z = (cols, cols)
        high, low = split(
            band(taps, rank, 2, iota(shape_z, 0) - iota(shape_z, 1) + half, reverse)
        )
        for copy in range(2):
            mat_z[rank, copy * cols : (copy + 1) * cols, :cols] = high
            mat_z[rank, copy * cols : (copy + 1) * cols, cols:] = low


def blur_xz(window, middle, mat_x, mat_z, planes, width, rows, cols):
    def first(step, carry):
        base = step * GROUP
        parts = []
        for k in range(GROUP // 2):
            sides = []
            for side in range(2):
                y = base + 2 * k + side
                high, low = split(window[pl.ds(y, width, stride=rows), :])
                sides.append(jnp.concatenate([high, low, high], axis=0))
            both = dot(mat_x[:, : 3 * width], jnp.concatenate(sides, axis=1))
            parts.append(both[:, :cols])
            parts.append(both[:, cols:])
        for rank in range(2):
            stack = jnp.concatenate(
                [p[rank * planes : (rank + 1) * planes] for p in parts], axis=0
            )
            high, low = split(stack)
            both = dot(jnp.concatenate([high, low], axis=1), mat_z[rank])
            result = both[:, :cols] + both[:, cols:]
            for k in range(GROUP):
                middle[pl.ds(rank * planes * rows + base + k, planes, stride=rows), :] = result[
                    k * planes : (k + 1) * planes
                ]
        return carry

    lax.fori_loop(0, rows // GROUP, first, 0)


def blur_y(middle, mat_y, planes, rows, cols, start, number, finish):
    def second(step, carry):
        x = start + 2 * step
        highs, lows = [], []
        for side in range(2):
            data = [
                middle[pl.ds(pl.multiple_of((rank * planes + x + side) * rows, 8), rows), :]
                for rank in range(2)
            ]
            high, low = split(jnp.concatenate(data, axis=0))
            highs.append(high)
            lows.append(low)
        both = dot(mat_y[...], jnp.concatenate(highs, axis=1))
        result = both[:rows] + both[rows:]
        result = result + dot(mat_y[:rows, :], jnp.concatenate(lows, axis=1))
        finish(2 * step, result[:, :cols])
        finish(2 * step + 1, result[:, cols:])
        return carry

    lax.fori_loop(0, number // 2, second, 0)


def encode(value):
    size = jnp.log(1.0 + jnp.abs(value) * (1.0 / KNEE)) * (1.0 / UNIT) + 0.5
    size = jnp.minimum(size, 32767.0)
    return jnp.where(value < 0.0, -size, size).astype(jnp.int32).astype(jnp.int16)


def decode(code):
    value = code.astype(jnp.int32).astype(jnp.float32)
    size = KNEE * (jnp.exp(UNIT * jnp.abs(value)) - 1.0)
    return jnp.where(value < 0.0, -size, size)


MESH = pl.DeviceIdType.MESH


def kernel(
    taps, weight, shifts, first, count, estimate, observed, out,
    window, middle, mats_x, mats_y, mats_z, extended, registered, mine,
    edge_out, edge_in, send, recv,
    seen_send, seen_recv, edge_send, edge_recv, sum_send, sum_recv,
):
    planes, rows, cols = estimate.shape
    width = planes + 2 * HALO
    blocks = lax.axis_size("blk")
    view = lax.axis_index("view")
    block = lax.axis_index("blk")
    partner = view + 1 - 2 * lax.rem(view, 2)
    inner = (view == 1) | (view == 2)
    outer = (view == 0) | (view == 3)
    has_low = block > 0
    has_high = block < blocks - 1
    starts = [0, planes // 2, PIECE, planes // 2 + PIECE]

    barrier = pltpu.get_barrier_semaphore()
    pl.semaphore_signal(barrier, inc=1, device_id={"view": partner}, device_id_type=MESH)

    @pl.when(inner)
    def _():
        pl.semaphore_signal(barrier, inc=1, device_id={"view": 3 - view}, device_id_type=MESH)

    @pl.when(has_low)
    def _():
        pl.semaphore_signal(barrier, inc=1, device_id={"blk": block - 1}, device_id_type=MESH)

    @pl.when(has_high)
    def _():
        pl.semaphore_signal(barrier, inc=1, device_id={"blk": block + 1}, device_id_type=MESH)

    def seen_copy(side):
        low = side == 0
        here = pl.ds(0, SHIFT_MAX) if low else pl.ds(planes - SHIFT_MAX, SHIFT_MAX)
        there = pl.ds(planes + SHIFT_MAX, SHIFT_MAX) if low else pl.ds(0, SHIFT_MAX)
        return pltpu.make_async_remote_copy(
            src_ref=observed.at[0, here],
            dst_ref=extended.at[there],
            send_sem=seen_send.at[side],
            recv_sem=seen_recv.at[side],
            device_id={"blk": block - 1 if low else block + 1},
            device_id_type=MESH,
        )

    def edge_copy(turn, piece):
        low = piece % 2 == 0
        place = (piece // 2) * PIECE
        return pltpu.make_async_remote_copy(
            src_ref=edge_out.at[turn, pl.ds(starts[piece], PIECE)],
            dst_ref=edge_in.at[turn, 1 if low else 0, pl.ds(place, PIECE)],
            send_sem=edge_send.at[turn, piece],
            recv_sem=edge_recv.at[turn, piece],
            device_id={"blk": block - 1 if low else block + 1},
            device_id_type=MESH,
        )

    def start_edge(turn, piece):
        @pl.when(has_low if piece % 2 == 0 else has_high)
        def _():
            edge_copy(turn, piece).start()

    def take_edges(turn):
        for piece in range(4):
            @pl.when(has_high if piece % 2 == 0 else has_low)
            def _():
                edge_copy(turn, piece).wait_recv()

        size = HALO * rows

        def body(place, carry):
            at = pl.multiple_of(place * rows, 8)
            window[pl.ds(at, rows), :] = edge_in[turn, 0, place].astype(jnp.float32)
            at = pl.multiple_of(size + (planes + place) * rows, 8)
            window[pl.ds(at, rows), :] = edge_in[turn, 1, place].astype(jnp.float32)
            return carry

        lax.fori_loop(0, HALO, body, 0)

    def set_own(turn, x, value):
        window[pl.ds(pl.multiple_of((HALO + x) * rows, 8), rows), :] = value
        edge_out[turn, x] = value.astype(jnp.bfloat16)

    def begin(x, carry):
        set_own(0, x, estimate[x])
        return carry

    lax.fori_loop(0, planes, begin, 0)

    @pl.when(block == 0)
    def _():
        extended[:SHIFT_MAX] = jnp.zeros((SHIFT_MAX, rows, cols), jnp.bfloat16)
        for turn in range(2 * ROUNDS):
            edge_in[turn, 0] = jnp.zeros((HALO, rows, cols), jnp.bfloat16)

    @pl.when(block == blocks - 1)
    def _():
        extended[planes + SHIFT_MAX :] = jnp.zeros((SHIFT_MAX, rows, cols), jnp.bfloat16)
        for turn in range(2 * ROUNDS):
            edge_in[turn, 1] = jnp.zeros((HALO, rows, cols), jnp.bfloat16)

    pl.semaphore_wait(
        barrier,
        1 + inner.astype(jnp.int32) + has_low.astype(jnp.int32) + has_high.astype(jnp.int32),
    )
    for piece in range(4):
        start_edge(0, piece)

    @pl.when(has_low)
    def _():
        seen_copy(0).start()

    @pl.when(has_high)
    def _():
        seen_copy(1).start()

    for way in range(2):
        blur_tables(
            taps, weight, planes, width, rows, cols, way == 1,
            mats_x.at[way], mats_y.at[way], mats_z.at[way],
        )
    extended[SHIFT_MAX : planes + SHIFT_MAX] = observed[0]
    covered = jnp.float32(0.0)
    owned = jnp.float32(0.0)
    for slot in range(first.shape[0]):
        inside = (block >= first[slot]) & (block < first[slot] + count[slot])
        covered = covered + jnp.where(inside, 1.0, 0.0)
        owned = owned + jnp.where(inside & (view == slot), 1.0, 0.0)
    share = jnp.full((rows, cols), owned, jnp.float32) / jnp.full((rows, cols), covered, jnp.float32)

    def register():
        @pl.when(has_high)
        def _():
            seen_copy(0).wait_recv()

        @pl.when(has_low)
        def _():
            seen_copy(1).wait_recv()

        shape_y, shape_z = (rows, rows), (cols, cols)
        shift_y = (iota(shape_y, 1) - iota(shape_y, 0) == shifts[0, 1]).astype(jnp.float32)
        shift_z = (iota(shape_z, 0) - iota(shape_z, 1) == shifts[0, 2]).astype(jnp.float32)
        shift_y, shift_z = shift_y.astype(jnp.bfloat16), shift_z.astype(jnp.bfloat16)

        def body(step, carry):
            x = 2 * step
            at = x + SHIFT_MAX + shifts[0, 0]
            both = jnp.concatenate([extended[at], extended[at + 1]], axis=0)
            both = dot(both, shift_z).astype(jnp.bfloat16)
            both = dot(shift_y, jnp.concatenate([both[:rows], both[rows:]], axis=1))
            registered[x] = both[:, :cols] + OFFSET
            registered[x + 1] = both[:, cols:] + OFFSET
            return carry

        lax.fori_loop(0, planes // 2, body, 0)

    def sum_copy(turn, stage, chunk):
        here = pl.ds(order[chunk], CHUNK)
        return pltpu.make_async_remote_copy(
            src_ref=send.at[turn, stage, here],
            dst_ref=recv.at[turn, stage, here],
            send_sem=sum_send.at[turn, stage, chunk],
            recv_sem=sum_recv.at[turn, stage, chunk],
            device_id={"view": 3 - view if stage == 1 else partner},
            device_id_type=MESH,
        )

    order = [start + part for start in starts for part in range(0, PIECE, CHUNK)]
    chunks = len(order)

    for turn in range(ROUNDS):
        mat_x, mat_y, mat_z = mats_x.at[0], mats_y.at[0], mats_z.at[0]
        take_edges(2 * turn)
        blur_xz(window, middle, mat_x, mat_z, planes, width, rows, cols)
        if turn == 0:
            register()
        for piece in range(4):
            def ratio(place, value):
                x = starts[piece] + place
                set_own(2 * turn + 1, x, registered[x] / (value + OFFSET))

            blur_y(middle, mat_y, planes, rows, cols, starts[piece], PIECE, ratio)
            start_edge(2 * turn + 1, piece)

        mat_x, mat_y, mat_z = mats_x.at[1], mats_y.at[1], mats_z.at[1]
        take_edges(2 * turn + 1)
        blur_xz(window, middle, mat_x, mat_z, planes, width, rows, cols)

        def produce(chunk):
            def give(place, value):
                log = share * jnp.log(value)
                mine[order[chunk] + place] = log
                send[turn, 0, order[chunk] + place] = encode(log)

            blur_y(middle, mat_y, planes, rows, cols, order[chunk], CHUNK, give)

            @pl.when(outer)
            def _():
                sum_copy(turn, 0, chunk).start()

        def add_pair(chunk):
            sum_copy(turn, 0, chunk).wait_recv()

            def body(place, carry):
                x = order[chunk] + place
                send[turn, 1, x] = encode(mine[x] + decode(recv[turn, 0, x]))
                return carry

            lax.fori_loop(0, CHUNK, body, 0)
            sum_copy(turn, 1, chunk).start()

        def update(x, code):
            old = estimate[x] if turn == 0 else out[x]
            new = old * jnp.exp(decode(code))
            out[x] = new
            if turn < ROUNDS - 1:
                set_own(2 * turn + 2, x, new)

        def pass_on(chunk):
            if turn < ROUNDS - 1 and chunk % 2 == 1:
                start_edge(2 * turn + 2, chunk // 2)

        def add_across(chunk):
            sum_copy(turn, 1, chunk).wait_recv()

            def body(place, carry):
                x = order[chunk] + place
                send[turn, 2, x] = encode(decode(send[turn, 1, x]) + decode(recv[turn, 1, x]))
                return carry

            lax.fori_loop(0, CHUNK, body, 0)
            sum_copy(turn, 2, chunk).start()

            def apply(place, carry):
                x = order[chunk] + place
                update(x, send[turn, 2, x])
                return carry

            lax.fori_loop(0, CHUNK, apply, 0)
            pass_on(chunk)

        def take_total(chunk):
            sum_copy(turn, 2, chunk).wait_recv()

            def apply(place, carry):
                x = order[chunk] + place
                update(x, recv[turn, 2, x])
                return carry

            lax.fori_loop(0, CHUNK, apply, 0)
            pass_on(chunk)

        for chunk in range(chunks):
            produce(chunk)
            if chunk % 4 == 3:
                @pl.when(inner)
                def _():
                    add_pair(chunk // 4)

        @pl.when(inner)
        def _():
            for chunk in range(2, chunks):
                add_pair(chunk)
                add_across(chunk - 2)
            add_across(chunks - 2)
            add_across(chunks - 1)

        @pl.when(outer)
        def _():
            for chunk in range(chunks):
                take_total(chunk)

    @pl.when(has_low)
    def _():
        seen_copy(0).wait_send()
        for turn in range(2 * ROUNDS):
            edge_copy(turn, 0).wait_send()
            edge_copy(turn, 2).wait_send()

    @pl.when(has_high)
    def _():
        seen_copy(1).wait_send()
        for turn in range(2 * ROUNDS):
            edge_copy(turn, 1).wait_send()
            edge_copy(turn, 3).wait_send()

    for turn in range(ROUNDS):
        @pl.when(outer)
        def _():
            for chunk in range(chunks):
                sum_copy(turn, 0, chunk).wait_send()

        @pl.when(inner)
        def _():
            for chunk in range(chunks):
                sum_copy(turn, 1, chunk).wait_send()
                sum_copy(turn, 2, chunk).wait_send()


def on_device(estimate, observed, psf_taps, psf_weight, shifts, cover_first, cover_count):
    planes, rows, cols = estimate.shape
    width = planes + 2 * HALO
    smem = pl.BlockSpec(memory_space=pltpu.SMEM)
    vmem = pl.BlockSpec(memory_space=pltpu.VMEM)
    dma = pltpu.SemaphoreType.DMA
    return pl.pallas_call(
        kernel,
        out_shape=jax.ShapeDtypeStruct(estimate.shape, jnp.float32),
        in_specs=[smem] * 5 + [vmem] * 2,
        out_specs=vmem,
        scratch_shapes=[
            pltpu.VMEM(((width + 1) * rows, cols), jnp.float32),
            pltpu.VMEM(((2 * planes + 1) * rows, cols), jnp.float32),
            pltpu.VMEM((2, 2 * planes, 4 * width), jnp.bfloat16),
            pltpu.VMEM((2, 2 * rows, 2 * rows), jnp.bfloat16),
            pltpu.VMEM((2, 2, 2 * cols, 2 * cols), jnp.bfloat16),
            pltpu.VMEM((planes + 2 * SHIFT_MAX, rows, cols), jnp.bfloat16),
            pltpu.VMEM((planes, rows, cols), jnp.float32),
            pltpu.VMEM((planes, rows, cols), jnp.float32),
            pltpu.VMEM((2 * ROUNDS, planes, rows, cols), jnp.bfloat16),
            pltpu.VMEM((2 * ROUNDS, 2, HALO, rows, cols), jnp.bfloat16),
            pltpu.VMEM((ROUNDS, 3, planes, rows, cols), jnp.int16),
            pltpu.VMEM((ROUNDS, 3, planes, rows, cols), jnp.int16),
            dma((2,)),
            dma((2,)),
            dma((2 * ROUNDS, 4)),
            dma((2 * ROUNDS, 4)),
            dma((ROUNDS, 3, planes // CHUNK)),
            dma((ROUNDS, 3, planes // CHUNK)),
        ],
        compiler_params=pltpu.CompilerParams(
            vmem_limit_bytes=56 * 2**20, collective_id=0, has_side_effects=True
        ),
        cost_estimate=pl.CostEstimate(
            flops=48 * planes * rows * cols * 3 * cols,
            bytes_accessed=12 * planes * rows * cols,
            transcendentals=0,
        ),
    )(psf_taps[0], psf_weight[0], shifts, cover_first, cover_count, estimate, observed)


def solution(mesh):
    placed = (
        P("blk", None, None),
        P("view", "blk", None, None),
        P("view", None, None, None),
        P("view", None),
        P("view", None),
        P(),
        P(),
    )
    return jax.shard_map(
        on_device, mesh=mesh, in_specs=placed, out_specs=P("blk", None, None), check_vma=False
    )
```

```python
import math

import jax
import jax.numpy as jnp
from jax import lax
from jax.experimental import pallas as pl
from jax.experimental.pallas import tpu as pltpu
from jax.sharding import PartitionSpec as P

SHIFT_MAX = 8
ROUNDS = 2
HALF_TAPS = 15
HALO = 16
OFFSET = 0.1
GROUP = 32
CHUNK = 2
PIECE = 4
KNEE = 0.05
LIMIT = 24.0
UNIT = math.log(1.0 + LIMIT / KNEE) / 32767.0


def split(value):
    high = value.astype(jnp.bfloat16)
    low = (value - high.astype(jnp.float32)).astype(jnp.bfloat16)
    return high, low


def dot(a, b):
    return jnp.dot(a, b, preferred_element_type=jnp.float32)


def band(taps, rank, factor, diff, reverse):
    count = taps.shape[2]
    matrix = jnp.zeros(diff.shape, jnp.float32)
    total = jnp.float32(0.0)
    for place in range(count):
        tap = taps[rank, factor, count - 1 - place if reverse else place]
        total = total + tap
        matrix = jnp.where(diff == place, tap, matrix)
    return matrix / jnp.full(diff.shape, total, jnp.float32)


def iota(shape, dim):
    return lax.broadcasted_iota(jnp.int32, shape, dim)


def blur_tables(taps, weight, planes, width, rows, cols, reverse, mat_x, mat_y, mat_z):
    half = HALF_TAPS
    weight_sum = weight[0] + weight[1]
    shape = (planes, 4 * width)
    column = iota(shape, 1)
    middle = column - width + HALO
    last = column - width - planes
    source = jnp.where(column < width, column, jnp.where(last < 0, middle, last))
    diff = source - iota(shape, 0) - (HALO - half)
    for rank in range(2):
        scale = jnp.full(shape, weight[rank], jnp.float32) / jnp.full(shape, weight_sum, jnp.float32)
        full = band(taps, rank, 0, diff, reverse) * scale
        high = full.astype(jnp.bfloat16).astype(jnp.float32)
        mixed = jnp.where(last < 0, high, jnp.where(last < width, full - high, 0.0))
        mat_x[rank * planes : (rank + 1) * planes, :] = mixed.astype(jnp.bfloat16)
        shape_y = (rows, rows)
        high, low = split(
            band(taps, rank, 1, iota(shape_y, 1) - iota(shape_y, 0) + half, reverse)
        )
        mat_y[:rows, rank * rows : (rank + 1) * rows] = high
        mat_y[rows:, rank * rows : (rank + 1) * rows] = low
        shape_z = (cols, cols)
        high, low = split(
            band(taps, rank, 2, iota(shape_z, 0) - iota(shape_z, 1) + half, reverse)
        )
        for copy in range(2):
            mat_z[rank, copy * cols : (copy + 1) * cols, :cols] = high
            mat_z[rank, copy * cols : (copy + 1) * cols, cols:] = low


def blur_xz(window, middle, mat_x, mat_z, planes, width, rows, cols):
    def first(step, carry):
        base = step * GROUP
        parts = []
        for k in range(GROUP // 2):
            sides = []
            for side in range(2):
                y = base + 2 * k + side
                high, low = split(window[pl.ds(y, width, stride=rows), :])
                low = low[HALO : HALO + planes]
                sides.append(jnp.concatenate([high, low, high], axis=0))
            both = dot(mat_x[:, : 2 * width + planes], jnp.concatenate(sides, axis=1))
            parts.append(both[:, :cols])
            parts.append(both[:, cols:])
        for rank in range(2):
            stack = jnp.concatenate(
                [p[rank * planes : (rank + 1) * planes] for p in parts], axis=0
            )
            high, low = split(stack)
            both = dot(jnp.concatenate([high, low], axis=1), mat_z[rank])
            result = both[:, :cols] + both[:, cols:]
            for k in range(GROUP):
                middle[pl.ds(rank * planes * rows + base + k, planes, stride=rows), :] = result[
                    k * planes : (k + 1) * planes
                ]
        return carry

    lax.fori_loop(0, rows // GROUP, first, 0)


def blur_y(middle, mat_y, planes, rows, cols, start, number, finish):
    for step in range(number // 2):
        highs, lows = [], []
        for side in range(2):
            x = start + 2 * step + side
            data = [
                middle[(rank * planes + x) * rows : (rank * planes + x + 1) * rows, :]
                for rank in range(2)
            ]
            high, low = split(jnp.concatenate(data, axis=0))
            highs.append(high)
            lows.append(low)
        both = dot(mat_y[...], jnp.concatenate(highs, axis=1))
        result = both[:rows] + both[rows:]
        result = result + dot(mat_y[:rows, :], jnp.concatenate(lows, axis=1))
        finish(2 * step, result[:, :cols])
        finish(2 * step + 1, result[:, cols:])


def encode(value):
    size = jnp.log(1.0 + jnp.abs(value) * (1.0 / KNEE)) * (1.0 / UNIT) + 0.5
    size = jnp.minimum(size, 32767.0)
    return jnp.where(value < 0.0, -size, size).astype(jnp.int32).astype(jnp.int16)


def decode(code):
    value = code.astype(jnp.int32).astype(jnp.float32)
    size = KNEE * (jnp.exp(UNIT * jnp.abs(value)) - 1.0)
    return jnp.where(value < 0.0, -size, size)


MESH = pl.DeviceIdType.MESH


def kernel(
    taps, weight, shifts, first, count, estimate, observed, out,
    window, middle, mats_x, mats_y, mats_z, extended, registered, mine,
    edge_out, edge_in, send, recv,
    seen_send, seen_recv, edge_send, edge_recv, sum_send, sum_recv,
):
    planes, rows, cols = estimate.shape
    width = planes + 2 * HALO
    blocks = lax.axis_size("blk")
    view = lax.axis_index("view")
    block = lax.axis_index("blk")
    partner = view + 1 - 2 * lax.rem(view, 2)
    inner = (view == 1) | (view == 2)
    outer = (view == 0) | (view == 3)
    has_low = block > 0
    has_high = block < blocks - 1
    starts = [side + place for place in range(0, HALO, PIECE) for side in (0, planes - HALO)]
    pieces = len(starts)

    barrier = pltpu.get_barrier_semaphore()
    pl.semaphore_signal(barrier, inc=1, device_id={"view": partner}, device_id_type=MESH)

    @pl.when(inner)
    def _():
        pl.semaphore_signal(barrier, inc=1, device_id={"view": 3 - view}, device_id_type=MESH)

    @pl.when(has_low)
    def _():
        pl.semaphore_signal(barrier, inc=1, device_id={"blk": block - 1}, device_id_type=MESH)

    @pl.when(has_high)
    def _():
        pl.semaphore_signal(barrier, inc=1, device_id={"blk": block + 1}, device_id_type=MESH)

    def seen_copy(side):
        low = side == 0
        here = pl.ds(0, SHIFT_MAX) if low else pl.ds(planes - SHIFT_MAX, SHIFT_MAX)
        there = pl.ds(planes + SHIFT_MAX, SHIFT_MAX) if low else pl.ds(0, SHIFT_MAX)
        return pltpu.make_async_remote_copy(
            src_ref=observed.at[0, here],
            dst_ref=extended.at[there],
            send_sem=seen_send.at[side],
            recv_sem=seen_recv.at[side],
            device_id={"blk": block - 1 if low else block + 1},
            device_id_type=MESH,
        )

    def edge_copy(turn, piece):
        low = piece % 2 == 0
        place = (piece // 2) * PIECE
        return pltpu.make_async_remote_copy(
            src_ref=edge_out.at[turn, pl.ds(starts[piece], PIECE)],
            dst_ref=edge_in.at[turn, 1 if low else 0, pl.ds(place, PIECE)],
            send_sem=edge_send.at[turn, piece],
            recv_sem=edge_recv.at[turn, piece],
            device_id={"blk": block - 1 if low else block + 1},
            device_id_type=MESH,
        )

    def start_edge(turn, piece):
        @pl.when(has_low if piece % 2 == 0 else has_high)
        def _():
            edge_copy(turn, piece).start()

    def take_edges(turn):
        for piece in range(pieces):
            @pl.when(has_high if piece % 2 == 0 else has_low)
            def _():
                edge_copy(turn, piece).wait_recv()

        size = HALO * rows

        def body(place, carry):
            at = pl.multiple_of(place * rows, 8)
            window[pl.ds(at, rows), :] = edge_in[turn, 0, place].astype(jnp.float32)
            at = pl.multiple_of(size + (planes + place) * rows, 8)
            window[pl.ds(at, rows), :] = edge_in[turn, 1, place].astype(jnp.float32)
            return carry

        lax.fori_loop(0, HALO, body, 0)

    def set_own(turn, x, value):
        window[pl.ds(pl.multiple_of((HALO + x) * rows, 8), rows), :] = value
        edge_out[turn, x] = value.astype(jnp.bfloat16)

    def begin(x, carry):
        set_own(0, x, estimate[x])
        return carry

    lax.fori_loop(0, planes, begin, 0)

    @pl.when(block == 0)
    def _():
        extended[:SHIFT_MAX] = jnp.zeros((SHIFT_MAX, rows, cols), jnp.bfloat16)
        for turn in range(2 * ROUNDS):
            edge_in[turn, 0] = jnp.zeros((HALO, rows, cols), jnp.bfloat16)

    @pl.when(block == blocks - 1)
    def _():
        extended[planes + SHIFT_MAX :] = jnp.zeros((SHIFT_MAX, rows, cols), jnp.bfloat16)
        for turn in range(2 * ROUNDS):
            edge_in[turn, 1] = jnp.zeros((HALO, rows, cols), jnp.bfloat16)

    pl.semaphore_wait(
        barrier,
        1 + inner.astype(jnp.int32) + has_low.astype(jnp.int32) + has_high.astype(jnp.int32),
    )

    @pl.when(has_low)
    def _():
        seen_copy(0).start()

    @pl.when(has_high)
    def _():
        seen_copy(1).start()

    for piece in range(pieces):
        start_edge(0, piece)

    for way in range(2):
        blur_tables(
            taps, weight, planes, width, rows, cols, way == 1,
            mats_x.at[way], mats_y.at[way], mats_z.at[way],
        )
    extended[SHIFT_MAX : planes + SHIFT_MAX] = observed[0]
    covered = jnp.float32(0.0)
    owned = jnp.float32(0.0)
    for slot in range(first.shape[0]):
        inside = (block >= first[slot]) & (block < first[slot] + count[slot])
        covered = covered + jnp.where(inside, 1.0, 0.0)
        owned = owned + jnp.where(inside & (view == slot), 1.0, 0.0)
    share = jnp.full((rows, cols), owned, jnp.float32) / jnp.full((rows, cols), covered, jnp.float32)

    def register():
        @pl.when(has_high)
        def _():
            seen_copy(0).wait_recv()

        @pl.when(has_low)
        def _():
            seen_copy(1).wait_recv()

        shape_y, shape_z = (rows, rows), (cols, cols)
        shift_y = (iota(shape_y, 1) - iota(shape_y, 0) == shifts[0, 1]).astype(jnp.float32)
        shift_z = (iota(shape_z, 0) - iota(shape_z, 1) == shifts[0, 2]).astype(jnp.float32)
        shift_y, shift_z = shift_y.astype(jnp.bfloat16), shift_z.astype(jnp.bfloat16)

        def body(step, carry):
            x = 2 * step
            at = x + SHIFT_MAX + shifts[0, 0]
            both = jnp.concatenate([extended[at], extended[at + 1]], axis=0)
            both = dot(both, shift_z).astype(jnp.bfloat16)
            both = dot(shift_y, jnp.concatenate([both[:rows], both[rows:]], axis=1))
            registered[x] = both[:, :cols] + OFFSET
            registered[x + 1] = both[:, cols:] + OFFSET
            return carry

        lax.fori_loop(0, planes // 2, body, 0)

    def sum_copy(turn, stage, chunk):
        here = pl.ds(order[chunk], CHUNK)
        return pltpu.make_async_remote_copy(
            src_ref=send.at[turn, stage, here],
            dst_ref=recv.at[turn, stage, here],
            send_sem=sum_send.at[turn, stage, chunk],
            recv_sem=sum_recv.at[turn, stage, chunk],
            device_id={"view": 3 - view if stage == 1 else partner},
            device_id_type=MESH,
        )

    order = [start + part for start in starts for part in range(0, PIECE, CHUNK)]
    chunks = len(order)
    each = PIECE // CHUNK

    for turn in range(ROUNDS):
        mat_x, mat_y, mat_z = mats_x.at[0], mats_y.at[0], mats_z.at[0]
        if turn == 0:
            register()
        take_edges(2 * turn)
        blur_xz(window, middle, mat_x, mat_z, planes, width, rows, cols)
        for piece in range(pieces):
            def ratio(place, value):
                x = starts[piece] + place
                set_own(2 * turn + 1, x, registered[x] / (value + OFFSET))

            blur_y(middle, mat_y, planes, rows, cols, starts[piece], PIECE, ratio)
            start_edge(2 * turn + 1, piece)

        mat_x, mat_y, mat_z = mats_x.at[1], mats_y.at[1], mats_z.at[1]
        take_edges(2 * turn + 1)
        blur_xz(window, middle, mat_x, mat_z, planes, width, rows, cols)

        def produce(piece):
            def give(place, value):
                log = share * jnp.log(value)
                mine[starts[piece] + place] = log
                send[turn, 0, starts[piece] + place] = encode(log)

            blur_y(middle, mat_y, planes, rows, cols, starts[piece], PIECE, give)

            @pl.when(outer)
            def _():
                for part in range(each):
                    sum_copy(turn, 0, each * piece + part).start()

        def add_pair(chunk):
            sum_copy(turn, 0, chunk).wait_recv()

            def body(place, carry):
                x = order[chunk] + place
                send[turn, 1, x] = encode(mine[x] + decode(recv[turn, 0, x]))
                return carry

            lax.fori_loop(0, CHUNK, body, 0, unroll=True)
            sum_copy(turn, 1, chunk).start()

        def update(x, code):
            old = estimate[x] if turn == 0 else out[x]
            new = old * jnp.exp(decode(code))
            out[x] = new
            if turn < ROUNDS - 1:
                set_own(2 * turn + 2, x, new)

        def pass_on(chunk):
            if turn < ROUNDS - 1 and chunk % each == each - 1:
                start_edge(2 * turn + 2, chunk // each)

        def add_across(chunk):
            sum_copy(turn, 1, chunk).wait_recv()

            def body(place, carry):
                x = order[chunk] + place
                send[turn, 2, x] = encode(decode(send[turn, 1, x]) + decode(recv[turn, 1, x]))
                return carry

            lax.fori_loop(0, CHUNK, body, 0, unroll=True)
            sum_copy(turn, 2, chunk).start()

            def apply(place, carry):
                x = order[chunk] + place
                update(x, send[turn, 2, x])
                return carry

            lax.fori_loop(0, CHUNK, apply, 0, unroll=True)
            pass_on(chunk)

        def take_total(chunk):
            sum_copy(turn, 2, chunk).wait_recv()

            def apply(place, carry):
                x = order[chunk] + place
                update(x, recv[turn, 2, x])
                return carry

            lax.fori_loop(0, CHUNK, apply, 0, unroll=True)
            pass_on(chunk)

        for piece in range(pieces):
            produce(piece)
            if piece in (pieces // 2, pieces - 1):
                @pl.when(inner)
                def _():
                    add_pair(0 if piece < pieces - 1 else 1)

        @pl.when(inner)
        def _():
            for chunk in range(2, chunks):
                add_pair(chunk)
                add_across(chunk - 2)
            add_across(chunks - 2)
            add_across(chunks - 1)

        @pl.when(outer)
        def _():
            for chunk in range(chunks):
                take_total(chunk)

    @pl.when(has_low)
    def _():
        seen_copy(0).wait_send()
        for turn in range(2 * ROUNDS):
            for piece in range(0, pieces, 2):
                edge_copy(turn, piece).wait_send()

    @pl.when(has_high)
    def _():
        seen_copy(1).wait_send()
        for turn in range(2 * ROUNDS):
            for piece in range(1, pieces, 2):
                edge_copy(turn, piece).wait_send()

    for turn in range(ROUNDS):
        @pl.when(outer)
        def _():
            for chunk in range(chunks):
                sum_copy(turn, 0, chunk).wait_send()

        @pl.when(inner)
        def _():
            for chunk in range(chunks):
                sum_copy(turn, 1, chunk).wait_send()
                sum_copy(turn, 2, chunk).wait_send()


def on_device(estimate, observed, psf_taps, psf_weight, shifts, cover_first, cover_count):
    planes, rows, cols = estimate.shape
    width = planes + 2 * HALO
    smem = pl.BlockSpec(memory_space=pltpu.SMEM)
    vmem = pl.BlockSpec(memory_space=pltpu.VMEM)
    dma = pltpu.SemaphoreType.DMA
    return pl.pallas_call(
        kernel,
        out_shape=jax.ShapeDtypeStruct(estimate.shape, jnp.float32),
        in_specs=[smem] * 5 + [vmem] * 2,
        out_specs=vmem,
        scratch_shapes=[
            pltpu.VMEM(((width + 1) * rows, cols), jnp.float32),
            pltpu.VMEM(((2 * planes + 1) * rows, cols), jnp.float32),
            pltpu.VMEM((2, 2 * planes, 4 * width), jnp.bfloat16),
            pltpu.VMEM((2, 2 * rows, 2 * rows), jnp.bfloat16),
            pltpu.VMEM((2, 2, 2 * cols, 2 * cols), jnp.bfloat16),
            pltpu.VMEM((planes + 2 * SHIFT_MAX, rows, cols), jnp.bfloat16),
            pltpu.VMEM((planes, rows, cols), jnp.float32),
            pltpu.VMEM((planes, rows, cols), jnp.float32),
            pltpu.VMEM((2 * ROUNDS, planes, rows, cols), jnp.bfloat16),
            pltpu.VMEM((2 * ROUNDS, 2, HALO, rows, cols), jnp.bfloat16),
            pltpu.VMEM((ROUNDS, 3, planes, rows, cols), jnp.int16),
            pltpu.VMEM((ROUNDS, 3, planes, rows, cols), jnp.int16),
            dma((2,)),
            dma((2,)),
            dma((2 * ROUNDS, 2 * HALO // PIECE)),
            dma((2 * ROUNDS, 2 * HALO // PIECE)),
            dma((ROUNDS, 3, planes // CHUNK)),
            dma((ROUNDS, 3, planes // CHUNK)),
        ],
        compiler_params=pltpu.CompilerParams(
            vmem_limit_bytes=56 * 2**20, collective_id=0, has_side_effects=True
        ),
        cost_estimate=pl.CostEstimate(
            flops=48 * planes * rows * cols * 3 * cols,
            bytes_accessed=12 * planes * rows * cols,
            transcendentals=0,
        ),
    )(psf_taps[0], psf_weight[0], shifts, cover_first, cover_count, estimate, observed)


def solution(mesh):
    placed = (
        P("blk", None, None),
        P("view", "blk", None, None),
        P("view", None, None, None),
        P("view", None),
        P("view", None),
        P(),
        P(),
    )
    return jax.shard_map(
        on_device, mesh=mesh, in_specs=placed, out_specs=P("blk", None, None), check_vma=False
    )
```
